256 devices in a mesh: row: 8 (over y, core), col: 16 (over z_lo, x), dp: 2 (over z_hi).
Axes of the slice: x: 4, y: 4, z: 8 (z_hi: 2, z_lo: 4; z = z_hi * 4 + z_lo), core: 2. Of those that a mesh axis runs over, the one named last changes fastest.
Arguments:
- tokens: bfloat16 [640, 12288], P(('row', 'dp'), 'col'), may hold values from -6 to 6
- w_in: bfloat16 [12288, 24576], P('col', ('row', 'dp')), may hold values from -0.0546875 to 0.0546875
- w_out: bfloat16 [24576, 12288], P(('row', 'dp'), 'col'), may hold values from -0.0390625 to 0.0390625
- grad_out: bfloat16 [640, 12288], P(('row', 'dp'), 'col'), may hold values from -6 to 6
Outputs:
- output: float32 [640, 12288], P(('row', 'dp'), 'col')
- grad_tokens: float32 [640, 12288], P(('row', 'dp'), 'col')
- grad_w_in: bfloat16 [12288, 24576], P('col', ('row', 'dp'))
- grad_w_out: bfloat16 [24576, 12288], P(('row', 'dp'), 'col')
The draws below stay inside these ranges and needn't reach their ends.
All inputs are finite; a program needn't handle non-finite values.
Results may differ from the reference program's by a relative error of at most 0.0049.
Values may be sent and summed in bfloat16 or wider, within the bound.
No kernel may reach another device: no remote copies, remote signals or barrier semaphores. Data moves between devices by JAX's collectives and lax.ppermute only.
A program may use at most 128 MiB of HBM per device.

```python
import math
import jax
import jax.numpy as jnp

D = 12288
FF = 24576
TOKENS = 640


def level_of(stream_key, extent, split, smallest, largest):
    def one(axis_at, blocks):
        draws = jax.random.uniform(jax.random.fold_in(jax.random.fold_in(stream_key, 6), axis_at), (blocks,), jnp.float32, smallest / len(split), largest / len(split))
        return jnp.repeat(jnp.exp(draws), extent[axis_at] // blocks).reshape((-1,) + (1,) * (len(extent) - axis_at - 1))

    gain = one(*split[0])
    for cut in split[1:]:
        gain = gain * one(*cut)
    return gain


def noise(key, shape, scale, most, pieces=(), held_as=jnp.bfloat16):
    result = scale * jax.random.normal(key, shape, jnp.float32)
    if pieces:
        result = result * level_of(key, shape, pieces, -0.22, 0.18)
    return jnp.clip(result, -most, most).astype(held_as)


def setup_inputs(seed: int = 0) -> dict:
    arg_keys = jax.random.split(jax.random.key(seed), 5)
    tokens = noise(arg_keys[0], (TOKENS, D), 1.0, 6.0, ((0, 16), (1, 16)))
    w_in = noise(arg_keys[1], (D, FF), D ** -0.5, 0.0546875, ((0, 16), (1, 16)))
    w_out = noise(arg_keys[2], (FF, D), FF ** -0.5, 0.0390625, ((0, 16), (1, 16)))
    grad_out = noise(arg_keys[3], (TOKENS, D), 1.0, 6.0, ((0, 16), (1, 16)))
    return {"tokens": tokens, "w_in": w_in, "w_out": w_out, "grad_out": grad_out}


gelu_scale = math.sqrt(2.0 / math.pi)
cubic_coef = 0.044715

def gelu_parts(pre_act):
    inner_arg = gelu_scale * (pre_act + cubic_coef * pre_act * pre_act * pre_act)
    tanh_part = jnp.tanh(inner_arg)
    values = 0.5 * pre_act * (1.0 + tanh_part)
    slopes = 0.5 * (1.0 + tanh_part) + 0.5 * pre_act * (1.0 - tanh_part * tanh_part) * gelu_scale * (1.0 + 3.0 * cubic_coef * pre_act * pre_act)
    return (values, slopes)

def reference(tokens, w_in, w_out, grad_out):
    pre_act = jnp.dot(tokens, w_in, preferred_element_type=jnp.float32)
    values, slopes = gelu_parts(pre_act)
    activation = values.astype(jnp.bfloat16)
    output = tokens.astype(jnp.float32) + jnp.dot(activation, w_out, preferred_element_type=jnp.float32)
    backward = jnp.dot(grad_out, w_out.T, preferred_element_type=jnp.float32)
    grad_hidden = (backward * slopes).astype(jnp.bfloat16)
    grad_tokens = grad_out.astype(jnp.float32) + jnp.dot(grad_hidden, w_in.T, preferred_element_type=jnp.float32)
    grad_w_in = jnp.dot(tokens.T, grad_hidden, preferred_element_type=jnp.float32).astype(jnp.bfloat16)
    grad_w_out = jnp.dot(activation.T, grad_out, preferred_element_type=jnp.float32).astype(jnp.bfloat16)
    return (output, grad_tokens, grad_w_in, grad_w_out)
```

```python
import functools
import math

import jax
import jax.numpy as jnp
from jax import lax
from jax.experimental import pallas as pl
from jax.experimental.pallas import tpu as pltpu
from jax.sharding import Mesh
from jax.sharding import PartitionSpec as P

BF16, F32 = jnp.bfloat16, jnp.float32
GELU_SCALE = math.sqrt(2.0 / math.pi)
CUBIC = 0.044715
VMEM = pl.BlockSpec(memory_space=pltpu.VMEM)
SMEM = pl.BlockSpec(memory_space=pltpu.SMEM)
N = 4


def gelu_parts(v):
    t = jnp.tanh(GELU_SCALE * (v + CUBIC * v * v * v))
    values = 0.5 * v * (1.0 + t)
    slopes = 0.5 * (1.0 + t) + 0.5 * v * (1.0 - t * t) * GELU_SCALE * (
        1.0 + 3.0 * CUBIC * v * v
    )
    return values, slopes


def dot(a, b, contract_a, contract_b):
    return lax.dot_general(
        a, b, (((contract_a,), (contract_b,)), ((), ())), preferred_element_type=F32
    )


def call(body, outs, flops, traffic, *args):
    specs = [SMEM if a.dtype == jnp.int32 else VMEM for a in args]
    return pl.pallas_call(
        body,
        out_shape=[jax.ShapeDtypeStruct(s, d) for s, d in outs],
        in_specs=specs,
        out_specs=[VMEM] * len(outs),
        compiler_params=pltpu.CompilerParams(vmem_limit_bytes=28 << 20),
        cost_estimate=pl.CostEstimate(flops=flops, bytes_accessed=traffic, transcendentals=0),
    )(*args)


def first_products(at, mine, other, w_in, w_out, rows, keep, one, two, three):
    half = mine.shape[2]
    block = 2 * half
    for a in range(2):
        for d in range(N):
            k = lax.rem(at[0] + d, N)
            both = jnp.concatenate([mine[k, a].astype(F32), other[k, a].astype(F32)], axis=0)
            rows[a, d * block : (d + 1) * block] = both.astype(BF16)
    width = 512
    for n in range(w_in.shape[1] // width):
        cut = slice(n * width, (n + 1) * width)
        for a in range(2):
            if a == 0:
                part = dot(rows[0], w_in[:, cut], 1, 0)
            else:
                part = dot(rows[1], w_out[cut, :], 1, 1)
            keep[a, :, cut] = part[:block]
            for d, out in enumerate((one, two, three), 1):
                out[a, :, cut] = part[d * block : (d + 1) * block].astype(BF16)


def add_blocks(at, keep, one, two, three, mine, first, second, third):
    width = mine.shape[2]
    for e, out in enumerate((mine, first, second, third)):
        start = pl.multiple_of(lax.rem(at[1] + e, N) * width, 128)
        cut = pl.ds(start, width)
        for a in range(2):
            total = keep[a, :, cut]
            for got in (one, two, three):
                total = total + got[a, :, cut].astype(F32)
            out[a] = total.astype(out.dtype)


def activate(mine, one, two, three, out):
    def total(a):
        return (
            mine[a] + one[a].astype(F32) + two[a].astype(F32) + three[a].astype(F32)
        )

    values, slopes = gelu_parts(total(0))
    out[0] = values.astype(BF16)
    out[1] = (total(1) * slopes).astype(BF16)


def assemble(at, mine, one, two, three, out):
    width = mine.shape[2]
    for e, got in enumerate((mine, one, two, three)):
        start = pl.multiple_of(lax.rem(at[1] + N - e, N) * width, 128)
        for a in range(2):
            out[a, :, pl.ds(start, width)] = got[a]


def second_products(at, mine, one, two, three, w_in, w_out, hidden, keep, send):
    block = mine.shape[1]
    half = block // 2
    for a in range(2):
        for d, got in enumerate((mine, one, two, three)):
            hidden[a, d * block : (d + 1) * block] = got[a]
    for a in range(2):
        if a == 0:
            part = dot(hidden[0], w_out[...], 1, 0)
        else:
            part = dot(hidden[1], w_in[...], 1, 1)
        for d in range(N):
            k = lax.rem(at[0] + N - d, N)
            keep[k, a] = part[d * block : d * block + half]
            send[k, a] = part[d * block + half : (d + 1) * block].astype(BF16)


def add_halves(keep, got, *outs):
    for k, out in enumerate(outs):
        out[...] = (keep[k] + got[k].astype(F32)).astype(out.dtype)


def weight_grads(rows_own, hidden_own, rows_far, hidden_far, grad_in, grad_out, lhs, rhs):
    block = rows_own.shape[1] // N
    extent = rows_own.shape[1]
    for a in range(2):
        for i, (rows, hidden) in enumerate(((rows_own, hidden_own), (rows_far, hidden_far))):
            for d in range(N):
                f = (N - d) % N
                lhs[a, i * extent + d * block : i * extent + (d + 1) * block] = rows[
                    a, f * block : (f + 1) * block
                ]
            rhs[a, i * extent : (i + 1) * extent] = hidden[a]
    width = 256
    for n in range(grad_in.shape[0] // width):
        cut = slice(n * width, (n + 1) * width)
        grad_in[cut, :] = dot(lhs[0, :, cut], rhs[1], 0, 0).astype(BF16)
    for n in range(grad_out.shape[0] // width):
        cut = slice(n * width, (n + 1) * width)
        grad_out[cut, :] = dot(rhs[0, :, cut], lhs[1], 0, 0).astype(BF16)


def final_sum(tokens, grad_out, base, *rest):
    *parts, output, grad_tokens = rest
    for a, (source, out) in enumerate(((tokens, output), (grad_out, grad_tokens))):
        total = source[...].astype(F32) + base[a]
        for part in parts:
            total = total + part[a].astype(F32)
        out[...] = total


def shift(value, axis, step):
    return lax.ppermute(value, axis, [(i, (i + step) % N) for i in range(N)])


def swap(value, axis):
    return lax.ppermute(value, axis, [(0, 1), (1, 0)])


def shards(tokens, w_in, w_out, grad_out):
    half, width = tokens.shape
    hidden = w_in.shape[1]
    block = 2 * half
    cut = hidden // N
    at = jnp.stack([lax.axis_index("x"), lax.axis_index("zl")]).astype(jnp.int32)
    product_flops = 2 * 2 * N * block * width * hidden

    mine = jnp.stack([tokens, grad_out])
    own = jnp.stack([mine] + [shift(mine, "y", -k) for k in range(1, N)])
    far = swap(own, "zh")

    def middle(gathered):
        rows, keep, *send = call(
            first_products,
            [((2, N * block, width), BF16), ((2, block, hidden), F32)]
            + [((2, block, hidden), BF16)] * 3,
            product_flops,
            12 << 20,
            at, gathered, swap(gathered, "core"), w_in, w_out,
        )
        got = [shift(s, "x", d) for d, s in enumerate(send, 1)]
        keep, *send = call(
            add_blocks,
            [((2, block, cut), F32)] + [((2, block, cut), BF16)] * 3,
            1 << 20,
            4 << 20,
            at, keep, *got,
        )
        got = [shift(s, "zl", e) for e, s in enumerate(send, 1)]
        (piece,) = call(
            activate, [((2, block, cut), BF16)], 4 << 20, 1 << 20, keep, *got
        )
        got = [shift(piece, "zl", e) for e in range(1, N)]
        (wide,) = call(
            assemble, [((2, block, hidden), BF16)], 0, 1 << 20, at, piece, *got
        )
        got = [shift(wide, "x", d) for d in range(1, N)]
        hid, keep, send = call(
            second_products,
            [
                ((2, N * block, hidden), BF16),
                ((N, 2, half, width), F32),
                ((N, 2, half, width), BF16),
            ],
            product_flops,
            12 << 20,
            at, wide, *got, w_in, w_out,
        )
        return rows, hid, keep, swap(send, "core")

    rows_own, hid_own, keep, got = middle(own)
    base, *send = call(
        add_halves,
        [((2, half, width), F32)] + [((2, half, width), BF16)] * 3,
        1 << 18, 2 << 20, keep, got,
    )
    parts = [shift(s, "y", k) for k, s in enumerate(send, 1)]

    rows_far, hid_far, keep, got = middle(far)
    send = call(
        add_halves, [((2, half, width), BF16)] * 4, 1 << 18, 2 << 20, keep, got
    )
    for k, s in enumerate(send):
        pairs = [
            (y * 2 + z, (y + k) % N * 2 + 1 - z) for y in range(N) for z in range(2)
        ]
        parts.append(lax.ppermute(s, ("y", "zh"), pairs))

    grads = pl.pallas_call(
        weight_grads,
        out_shape=[
            jax.ShapeDtypeStruct((width, hidden), BF16),
            jax.ShapeDtypeStruct((hidden, width), BF16),
        ],
        in_specs=[VMEM] * 4,
        out_specs=[VMEM] * 2,
        scratch_shapes=[
            pltpu.VMEM((2, 2 * N * block, width), BF16),
            pltpu.VMEM((2, 2 * N * block, hidden), BF16),
        ],
        compiler_params=pltpu.CompilerParams(vmem_limit_bytes=36 << 20),
        cost_estimate=pl.CostEstimate(
            flops=2 * product_flops, bytes_accessed=12 << 20, transcendentals=0
        ),
    )(rows_own, hid_own, rows_far, hid_far)

    output, grad_tokens = call(
        final_sum,
        [((half, width), F32)] * 2,
        1 << 20, 2 << 20, tokens, grad_out, base, *parts,
    )
    return output, grad_tokens, grads[0], grads[1]


def solution(mesh):
    fine = Mesh(mesh.devices.reshape(4, 2, 4, 4, 2), ("y", "core", "zl", "x", "zh"))
    row, col = ("y", "core", "zh"), ("zl", "x")
    by_token, in_spec, out_spec = P(row, col), P(col, row), P(row, col)
    return jax.shard_map(
        shards,
        mesh=fine,
        in_specs=(by_token, in_spec, out_spec, by_token),
        out_specs=(by_token, by_token, in_spec, out_spec),
        check_vma=False,
    )
```

```python
import functools
import math

import jax
import jax.numpy as jnp
from jax import lax
from jax.experimental import pallas as pl
from jax.experimental.pallas import tpu as pltpu
from jax.sharding import Mesh
from jax.sharding import PartitionSpec as P

BF16, F32 = jnp.bfloat16, jnp.float32
GELU_SCALE = math.sqrt(2.0 / math.pi)
CUBIC = 0.044715
VMEM = pl.BlockSpec(memory_space=pltpu.VMEM)
SMEM = pl.BlockSpec(memory_space=pltpu.SMEM)
N = 4


def gelu_parts(v):
    t = jnp.tanh(GELU_SCALE * (v + CUBIC * v * v * v))
    values = 0.5 * v * (1.0 + t)
    slopes = 0.5 * (1.0 + t) + 0.5 * v * (1.0 - t * t) * GELU_SCALE * (
        1.0 + 3.0 * CUBIC * v * v
    )
    return values, slopes


def dot(a, b, contract_a, contract_b):
    return lax.dot_general(
        a, b, (((contract_a,), (contract_b,)), ((), ())), preferred_element_type=F32
    )


class Order:
    def __init__(self):
        self.last = None

    def call(self, body, outs, *args, limit=28, scratch=(), after=(), flops=0, traffic=0):
        anyplace = pl.BlockSpec(memory_space=pl.ANY)
        specs = [SMEM if a.dtype == jnp.int32 else VMEM for a in args]
        before = list(after) + ([] if self.last is None else [self.last])

        def ordered(*refs):
            ins, rest = refs[: len(args)], refs[len(args) + len(before) :]
            results, token, scratches = rest[: len(outs)], rest[len(outs)], rest[len(outs) + 1 :]
            body(*ins, *results, *scratches)
            token[...] = jnp.zeros_like(token)

        *results, self.last = pl.pallas_call(
            ordered,
            out_shape=[jax.ShapeDtypeStruct(s, d) for s, d in outs]
            + [jax.ShapeDtypeStruct((8, 128), F32)],
            in_specs=specs + [anyplace] * len(before),
            out_specs=[VMEM] * (len(outs) + 1),
            scratch_shapes=scratch,
            compiler_params=pltpu.CompilerParams(vmem_limit_bytes=limit << 20),
            cost_estimate=pl.CostEstimate(
                flops=flops, bytes_accessed=traffic, transcendentals=0
            ),
        )(*args, *before)
        return results


def first_products(at, mine, other, w_in, w_out, rows, keep, one, two, three):
    half = mine.shape[2]
    block = 2 * half
    for a in range(2):
        for d in range(N):
            k = lax.rem(at[0] + d, N)
            both = jnp.concatenate(
                [mine[k, a].astype(F32), other[k, a].astype(F32)], axis=0
            )
            rows[a, d * block : (d + 1) * block] = both.astype(BF16)
    width = 512
    for n in range(w_in.shape[1] // width):
        cut = slice(n * width, (n + 1) * width)
        for a in range(2):
            if a == 0:
                part = dot(rows[0], w_in[:, cut], 1, 0)
            else:
                part = dot(rows[1], w_out[cut, :], 1, 1)
            keep[a, :, cut] = part[:block]
            for d, out in enumerate((one, two, three), 1):
                out[a, :, cut] = part[d * block : (d + 1) * block].astype(BF16)


def add_blocks(at, keep, one, two, three, mine, first, second, third):
    width = mine.shape[2]
    for e, out in enumerate((mine, first, second, third)):
        start = pl.multiple_of(lax.rem(at[1] + e, N) * width, 128)
        cut = pl.ds(start, width)
        for a in range(2):
            total = keep[a, :, cut]
            for got in (one, two, three):
                total = total + got[a, :, cut].astype(F32)
            out[a] = total.astype(out.dtype)


def activate(mine, one, two, three, out):
    def total(a):
        return (
            mine[a] + one[a].astype(F32) + two[a].astype(F32) + three[a].astype(F32)
        )

    values, slopes = gelu_parts(total(0))
    out[0] = values.astype(BF16)
    out[1] = (total(1) * slopes).astype(BF16)


def assemble(at, mine, one, two, three, out):
    width = mine.shape[-1]
    for e, got in enumerate((mine, one, two, three)):
        start = pl.multiple_of(lax.rem(at[1] + N - e, N) * width, 128)
        for a in range(2):
            out[a, :, pl.ds(start, width)] = got[a]


def second_products(at, mine, one, two, three, w_in, w_out, hidden, keep, send):
    block = mine.shape[1]
    half = block // 2
    for a in range(2):
        for d, got in enumerate((mine, one, two, three)):
            hidden[a, d * block : (d + 1) * block] = got[a]
    for a in range(2):
        if a == 0:
            part = dot(hidden[0], w_out[...], 1, 0)
        else:
            part = dot(hidden[1], w_in[...], 1, 1)
        for d in range(N):
            k = lax.rem(at[0] + N - d, N)
            keep[k, a] = part[d * block : d * block + half]
            send[k, a] = part[d * block + half : (d + 1) * block].astype(BF16)


def add_halves(keep, got, base, *outs):
    for k, out in enumerate((base, *outs)):
        out[...] = (keep[k] + got[k].astype(F32)).astype(out.dtype)


def add_all(base, *refs):
    total = base[...]
    for got in refs[:-1]:
        total = total + got[...].astype(F32)
    refs[-1][...] = total.astype(BF16)


def weight_grad(rows, hidden, *rest, of_rows):
    *before, out, lhs = rest
    which = 0 if of_rows else 1
    block = rows.shape[1] // N
    for d in range(N):
        f = (N - d) % N
        lhs[d * block : (d + 1) * block] = rows[which, f * block : (f + 1) * block]
    width = 256
    for n in range(out.shape[0] // width):
        cut = slice(n * width, (n + 1) * width)
        if of_rows:
            part = dot(lhs[:, cut], hidden[1], 0, 0)
        else:
            part = dot(hidden[0, :, cut], lhs[...], 0, 0)
        if before:
            part = part + before[0][cut, :]
        out[cut, :] = part.astype(out.dtype)


def own_sum(tokens, grad_out, base, *refs):
    *parts, out = refs
    for a, source in enumerate((tokens, grad_out)):
        total = source[...].astype(F32) + base[a]
        for part in parts:
            total = total + part[a].astype(F32)
        out[a] = total


def final_sum(base, got, output, grad_tokens):
    for a, out in enumerate((output, grad_tokens)):
        out[...] = base[a] + got[a].astype(F32)


def keep_as_is(source, out):
    out[...] = source[...]


def shift(value, axis, step):
    return lax.ppermute(value, axis, [(i, (i + step) % N) for i in range(N)])


def swap(value, axis):
    return lax.ppermute(value, axis, [(0, 1), (1, 0)])


def shards(tokens, w_in, w_out, grad_out):
    half, width = tokens.shape
    hidden = w_in.shape[1]
    block = 2 * half
    cut = hidden // N
    at = jnp.stack([lax.axis_index("x"), lax.axis_index("zl")]).astype(jnp.int32)
    order = Order()
    product_flops = 4 * N * block * width * hidden

    mine = jnp.stack([tokens, grad_out])

    def send(values, axis):
        return [shift(s, axis, d) for d, s in enumerate(values, 1)]

    def first(rows):
        rows, keep, *out = order.call(
            first_products,
            [((2, N * block, width), BF16), ((2, block, hidden), F32)]
            + [((2, block, hidden), BF16)] * 3,
            at, rows, swap(rows, "core"), w_in, w_out,
        )
        return rows, keep, send(out, "x")

    def add(keep, got):
        keep, *out = order.call(
            add_blocks,
            [((2, block, cut), F32)] + [((2, block, cut), BF16)] * 3,
            at, keep, *got,
        )
        return keep, send(out, "zl")

    def act(keep, got):
        return order.call(activate, [((2, block, cut), BF16)], keep, *got)[0]

    def spread(wide):
        return [wide] + send([wide] * 3, "x")

    def second(wide, after=()):
        hid, keep, out = order.call(
            second_products,
            [
                ((2, N * block, hidden), BF16),
                ((N, 2, half, width), F32),
                ((N, 2, half, width), BF16),
            ],
            at, *wide, w_in, w_out, after=after,
        )
        return hid, keep, out

    part = ((2, half, width), BF16)

    def halves(keep, got):
        base, *out = order.call(
            add_halves, [((2, half, width), F32)] + [part] * 3, keep, swap(got, "core")
        )
        return base, send(out, "y")

    def grad(shape, of_rows, dtype, rows, hid, *before):
        return order.call(
            functools.partial(weight_grad, of_rows=of_rows),
            [(shape, dtype)],
            rows, hid, *before,
            scratch=[pltpu.VMEM(rows.shape[1:], BF16)],
        )[0]

    own = jnp.stack([mine] + [shift(mine, "y", -k) for k in range(1, N)])
    far = swap(own, "zh")
    rows_o, keep_o, got_o = first(own)
    (far,) = order.call(keep_as_is, [(far.shape, BF16)], far, after=got_o)
    rows_f, keep_f, got_f = first(far)
    keep_o, got_o = add(keep_o, got_o)
    piece_o = act(keep_o, got_o)
    got_o = send([piece_o] * 3, "zl")
    keep_f, got_f = add(keep_f, got_f)
    (wide_o,) = order.call(
        assemble, [((2, block, hidden), BF16)], at, piece_o, *got_o
    )
    wide_o = spread(wide_o)
    piece_f = act(keep_f, got_f)
    got_f = send([piece_f] * 3, "zl")
    hid_o, keep_o, got_o = second(wide_o, got_f)
    (wide_f,) = order.call(
        assemble, [((2, block, hidden), BF16)], at, piece_f, *got_f
    )
    wide_f = spread(wide_f)
    base, parts = halves(keep_o, got_o)
    (own_total,) = order.call(
        own_sum, [((2, half, width), F32)], tokens, grad_out, base, *parts
    )
    grad_in = grad((width, hidden), True, F32, rows_o, hid_o)
    grad_second = grad((hidden, width), False, F32, rows_o, hid_o)
    hid_f, keep_f, got_f = second(wide_f)
    base, parts = halves(keep_f, got_f)
    grad_in = grad((width, hidden), True, BF16, rows_f, hid_f, grad_in)
    (total,) = order.call(add_all, [part], base, *parts)
    got = swap(total, "zh")
    grad_second = grad((hidden, width), False, BF16, rows_f, hid_f, grad_second)
    output, grad_tokens = order.call(
        final_sum, [((half, width), F32)] * 2, own_total, got
    )
    return output, grad_tokens, grad_in, grad_second


def solution(mesh):
    fine = Mesh(mesh.devices.reshape(4, 2, 4, 4, 2), ("y", "core", "zl", "x", "zh"))
    row, col = ("y", "core", "zh"), ("zl", "x")
    by_token, in_spec, out_spec = P(row, col), P(col, row), P(row, col)
    return jax.shard_map(
        shards,
        mesh=fine,
        in_specs=(by_token, in_spec, out_spec, by_token),
        out_specs=(by_token, by_token, in_spec, out_spec),
        check_vma=False,
    )
```

```python
import functools
import math

import jax
import jax.numpy as jnp
from jax import lax
from jax.experimental import pallas as pl
from jax.experimental.pallas import tpu as pltpu
from jax.sharding import Mesh
from jax.sharding import PartitionSpec as P

BF16, F32 = jnp.bfloat16, jnp.float32
GELU_SCALE = math.sqrt(2.0 / math.pi)
CUBIC = 0.044715
VMEM = pl.BlockSpec(memory_space=pltpu.VMEM)
SMEM = pl.BlockSpec(memory_space=pltpu.SMEM)
N = 4


def gelu_parts(v):
    t = jnp.tanh(GELU_SCALE * (v + CUBIC * v * v * v))
    values = 0.5 * v * (1.0 + t)
    slopes = 0.5 * (1.0 + t) + 0.5 * v * (1.0 - t * t) * GELU_SCALE * (
        1.0 + 3.0 * CUBIC * v * v
    )
    return values, slopes


def dot(a, b, contract_a, contract_b):
    return lax.dot_general(
        a, b, (((contract_a,), (contract_b,)), ((), ())), preferred_element_type=F32
    )


class Order:
    def __init__(self):
        self.last = None

    def call(self, body, outs, *args, limit=28, scratch=(), after=(), flops=0, traffic=0):
        anyplace = pl.BlockSpec(memory_space=pl.ANY)
        specs = [SMEM if a.dtype == jnp.int32 else VMEM for a in args]
        before = list(after) + ([] if self.last is None else [self.last])

        def ordered(*refs):
            ins, rest = refs[: len(args)], refs[len(args) + len(before) :]
            results, token, scratches = rest[: len(outs)], rest[len(outs)], rest[len(outs) + 1 :]
            body(*ins, *results, *scratches)
            token[...] = jnp.zeros_like(token)

        *results, self.last = pl.pallas_call(
            ordered,
            out_shape=[jax.ShapeDtypeStruct(s, d) for s, d in outs]
            + [jax.ShapeDtypeStruct((8, 128), F32)],
            in_specs=specs + [anyplace] * len(before),
            out_specs=[VMEM] * (len(outs) + 1),
            scratch_shapes=scratch,
            compiler_params=pltpu.CompilerParams(vmem_limit_bytes=limit << 20),
            cost_estimate=pl.CostEstimate(
                flops=flops, bytes_accessed=traffic, transcendentals=0
            ),
        )(*args, *before)
        return results


def first_products(at, mine, other, w_in, w_out, rows, keep, one, two, three):
    half = mine.shape[2]
    block = 2 * half
    for a in range(2):
        for d in range(N):
            k = lax.rem(at[0] + d, N)
            both = jnp.concatenate(
                [mine[k, a].astype(F32), other[k, a].astype(F32)], axis=0
            )
            rows[a, d * block : (d + 1) * block] = both.astype(BF16)
    width = 512
    for n in range(w_in.shape[1] // width):
        cut = slice(n * width, (n + 1) * width)
        for a in range(2):
            if a == 0:
                part = dot(rows[0], w_in[:, cut], 1, 0)
            else:
                part = dot(rows[1], w_out[cut, :], 1, 1)
            keep[a, :, cut] = part[:block]
            for d, out in enumerate((one, two, three), 1):
                out[a, :, cut] = part[d * block : (d + 1) * block].astype(BF16)


def add_blocks(at, keep, one, two, three, mine, first, second, third):
    width = mine.shape[2]
    for e, out in enumerate((mine, first, second, third)):
        start = pl.multiple_of(lax.rem(at[1] + e, N) * width, 128)
        cut = pl.ds(start, width)
        for a in range(2):
            total = keep[a, :, cut]
            for got in (one, two, three):
                total = total + got[a, :, cut].astype(F32)
            out[a] = total.astype(out.dtype)


def activate(mine, one, two, three, out):
    def total(a):
        return (
            mine[a] + one[a].astype(F32) + two[a].astype(F32) + three[a].astype(F32)
        )

    values, slopes = gelu_parts(total(0))
    out[0] = values.astype(BF16)
    out[1] = (total(1) * slopes).astype(BF16)


def assemble(at, mine, one, two, three, out):
    width = mine.shape[-1]
    for e, got in enumerate((mine, one, two, three)):
        start = pl.multiple_of(lax.rem(at[1] + N - e, N) * width, 128)
        for a in range(2):
            out[a, :, pl.ds(start, width)] = got[a]


def second_products(at, mine, one, two, three, w_in, w_out, hidden, keep, send):
    block = mine.shape[1]
    half = block // 2
    for a in range(2):
        for d, got in enumerate((mine, one, two, three)):
            hidden[a, d * block : (d + 1) * block] = got[a]
    for a in range(2):
        if a == 0:
            part = dot(hidden[0], w_out[...], 1, 0)
        else:
            part = dot(hidden[1], w_in[...], 1, 1)
        for d in range(N):
            k = lax.rem(at[0] + N - d, N)
            keep[k, a] = part[d * block : d * block + half]
            send[k, a] = part[d * block + half : (d + 1) * block].astype(BF16)


def add_halves(keep, got, base, *outs):
    for k, out in enumerate((base, *outs)):
        out[...] = (keep[k] + got[k].astype(F32)).astype(out.dtype)


def add_all(base, *refs):
    total = base[...]
    for got in refs[:-1]:
        total = total + got[...].astype(F32)
    refs[-1][...] = total.astype(BF16)


def weight_grad(rows, hidden, *rest, of_rows):
    *before, out, lhs = rest
    which = 0 if of_rows else 1
    block = rows.shape[1] // N
    for d in range(N):
        f = (N - d) % N
        lhs[d * block : (d + 1) * block] = rows[which, f * block : (f + 1) * block]
    width = 256
    for n in range(out.shape[0] // width):
        cut = slice(n * width, (n + 1) * width)
        if of_rows:
            part = dot(lhs[:, cut], hidden[1], 0, 0)
        else:
            part = dot(hidden[0, :, cut], lhs[...], 0, 0)
        if before:
            part = part + before[0][cut, :]
        out[cut, :] = part.astype(out.dtype)


def own_sum(tokens, grad_out, base, *refs):
    *parts, out = refs
    for a, source in enumerate((tokens, grad_out)):
        total = source[...].astype(F32) + base[a]
        for part in parts:
            total = total + part[a].astype(F32)
        out[a] = total


def final_sum(base, got, output, grad_tokens):
    for a, out in enumerate((output, grad_tokens)):
        out[...] = base[a] + got[a].astype(F32)


def keep_as_is(source, out):
    out[...] = source[...]


def shift(value, axis, step):
    return lax.ppermute(value, axis, [(i, (i + step) % N) for i in range(N)])


def swap(value, axis):
    return lax.ppermute(value, axis, [(0, 1), (1, 0)])


def shards(tokens, w_in, w_out, grad_out):
    half, width = tokens.shape
    hidden = w_in.shape[1]
    block = 2 * half
    cut = hidden // N
    at = jnp.stack([lax.axis_index("x"), lax.axis_index("zl")]).astype(jnp.int32)
    order = Order()
    product_flops = 4 * N * block * width * hidden

    mine = jnp.stack([tokens, grad_out])

    def send(values, axis):
        return [shift(s, axis, d) for d, s in enumerate(values, 1)]

    def first(rows):
        rows, keep, *out = order.call(
            first_products,
            [((2, N * block, width), BF16), ((2, block, hidden), F32)]
            + [((2, block, hidden), BF16)] * 3,
            at, rows, swap(rows, "core"), w_in, w_out,
        )
        return rows, keep, send(out, "x")

    def add(keep, got):
        keep, *out = order.call(
            add_blocks,
            [((2, block, cut), F32)] + [((2, block, cut), BF16)] * 3,
            at, keep, *got,
        )
        return keep, send(out, "zl")

    def act(keep, got):
        return order.call(activate, [((2, block, cut), BF16)], keep, *got)[0]

    def spread(wide):
        return [wide] + send([wide] * 3, "x")

    def second(wide, after=()):
        hid, keep, out = order.call(
            second_products,
            [
                ((2, N * block, hidden), BF16),
                ((N, 2, half, width), F32),
                ((N, 2, half, width), BF16),
            ],
            at, *wide, w_in, w_out, after=after,
        )
        return hid, keep, out

    part = ((2, half, width), BF16)

    def halves(keep, got):
        base, *out = order.call(
            add_halves, [((2, half, width), F32)] + [part] * 3, keep, swap(got, "core")
        )
        return base, send(out, "y")

    def grad(shape, of_rows, dtype, rows, hid, *before):
        return order.call(
            functools.partial(weight_grad, of_rows=of_rows),
            [(shape, dtype)],
            rows, hid, *before,
            flops=product_flops // 2, traffic=8 << 20,
            scratch=[pltpu.VMEM(rows.shape[1:], BF16)],
        )[0]

    own = jnp.stack([mine] + [shift(mine, "y", -k) for k in range(1, N)])
    far = swap(own, "zh")
    rows_o, keep_o, got_o = first(own)
    (far,) = order.call(keep_as_is, [(far.shape, BF16)], far, after=got_o)
    rows_f, keep_f, got_f = first(far)
    keep_o, got_o = add(keep_o, got_o)
    piece_o = act(keep_o, got_o)
    got_o = send([piece_o] * 3, "zl")
    keep_f, got_f = add(keep_f, got_f)
    (wide_o,) = order.call(
        assemble, [((2, block, hidden), BF16)], at, piece_o, *got_o
    )
    wide_o = spread(wide_o)
    piece_f = act(keep_f, got_f)
    got_f = send([piece_f] * 3, "zl")
    (wide_f,) = order.call(
        assemble, [((2, block, hidden), BF16)], at, piece_f, *got_f, after=wide_o[1:]
    )
    wide_f = spread(wide_f)
    hid_o, keep_o, got_o = second(wide_o)
    grad_in = grad((width, hidden), True, F32, rows_o, hid_o)
    grad_second = grad((hidden, width), False, F32, rows_o, hid_o)
    base, parts = halves(keep_o, got_o)
    (own_total,) = order.call(
        own_sum, [((2, half, width), F32)], tokens, grad_out, base, *parts
    )
    hid_f, keep_f, got_f = second(wide_f)
    base, parts = halves(keep_f, got_f)
    grad_in = grad((width, hidden), True, BF16, rows_f, hid_f, grad_in)
    (total,) = order.call(add_all, [part], base, *parts)
    got = swap(total, "zh")
    grad_second = grad((hidden, width), False, BF16, rows_f, hid_f, grad_second)
    output, grad_tokens = order.call(
        final_sum, [((half, width), F32)] * 2, own_total, got
    )
    return output, grad_tokens, grad_in, grad_second


def solution(mesh):
    fine = Mesh(mesh.devices.reshape(4, 2, 4, 4, 2), ("y", "core", "zl", "x", "zh"))
    row, col = ("y", "core", "zh"), ("zl", "x")
    by_token, in_spec, out_spec = P(row, col), P(col, row), P(row, col)
    return jax.shard_map(
        shards,
        mesh=fine,
        in_specs=(by_token, in_spec, out_spec, by_token),
        out_specs=(by_token, by_token, in_spec, out_spec),
        check_vma=False,
    )
```

```python
import functools
import math

import jax
import jax.numpy as jnp
from jax import lax
from jax.experimental import pallas as pl
from jax.experimental.pallas import tpu as pltpu
from jax.sharding import Mesh
from jax.sharding import PartitionSpec as P

BF16, F32 = jnp.bfloat16, jnp.float32
GELU_SCALE = math.sqrt(2.0 / math.pi)
CUBIC = 0.044715
VMEM = pl.BlockSpec(memory_space=pltpu.VMEM)
SMEM = pl.BlockSpec(memory_space=pltpu.SMEM)
N = 4


def gelu_parts(v):
    t = jnp.tanh(GELU_SCALE * (v + CUBIC * v * v * v))
    values = 0.5 * v * (1.0 + t)
    slopes = 0.5 * (1.0 + t) + 0.5 * v * (1.0 - t * t) * GELU_SCALE * (
        1.0 + 3.0 * CUBIC * v * v
    )
    return values, slopes


def dot(a, b, contract_a, contract_b):
    return lax.dot_general(
        a, b, (((contract_a,), (contract_b,)), ((), ())), preferred_element_type=F32
    )


class Order:
    def __init__(self):
        self.last = None

    def call(self, body, outs, *args, limit=28, scratch=(), after=(), flops=0, traffic=0):
        anyplace = pl.BlockSpec(memory_space=pl.ANY)
        specs = [SMEM if a.dtype == jnp.int32 else VMEM for a in args]
        before = list(after) + ([] if self.last is None else [self.last])

        def ordered(*refs):
            ins, rest = refs[: len(args)], refs[len(args) + len(before) :]
            results, token, scratches = rest[: len(outs)], rest[len(outs)], rest[len(outs) + 1 :]
            body(*ins, *results, *scratches)
            token[...] = jnp.zeros_like(token)

        *results, self.last = pl.pallas_call(
            ordered,
            out_shape=[jax.ShapeDtypeStruct(s, d) for s, d in outs]
            + [jax.ShapeDtypeStruct((8, 128), F32)],
            in_specs=specs + [anyplace] * len(before),
            out_specs=[VMEM] * (len(outs) + 1),
            scratch_shapes=scratch,
            compiler_params=pltpu.CompilerParams(vmem_limit_bytes=limit << 20),
            cost_estimate=pl.CostEstimate(
                flops=flops, bytes_accessed=traffic, transcendentals=0
            ),
        )(*args, *before)
        return results


def first_products(at, mine, other, w_in, w_out, rows, keep, one, two, three):
    half = mine.shape[2]
    block = 2 * half
    for a in range(2):
        for d in range(N):
            k = lax.rem(at[0] + d, N)
            both = jnp.concatenate(
                [mine[k, a].astype(F32), other[k, a].astype(F32)], axis=0
            )
            rows[a, d * block : (d + 1) * block] = both.astype(BF16)
    width = 512
    for n in range(w_in.shape[1] // width):
        cut = slice(n * width, (n + 1) * width)
        for a in range(2):
            if a == 0:
                part = dot(rows[0], w_in[:, cut], 1, 0)
            else:
                part = dot(rows[1], w_out[cut, :], 1, 1)
            keep[a, :, cut] = part[:block]
            for d, out in enumerate((one, two, three), 1):
                out[a, :, cut] = part[d * block : (d + 1) * block].astype(BF16)


def add_blocks(at, keep, one, two, three, mine, first, second, third):
    width = mine.shape[2]
    for e, out in enumerate((mine, first, second, third)):
        start = pl.multiple_of(lax.rem(at[1] + e, N) * width, 128)
        cut = pl.ds(start, width)
        for a in range(2):
            total = keep[a, :, cut]
            for got in (one, two, three):
                total = total + got[a, :, cut].astype(F32)
            out[a] = total.astype(out.dtype)


def activate(mine, one, two, three, out):
    def total(a):
        return (
            mine[a] + one[a].astype(F32) + two[a].astype(F32) + three[a].astype(F32)
        )

    values, slopes = gelu_parts(total(0))
    out[0] = values.astype(BF16)
    out[1] = (total(1) * slopes).astype(BF16)


def assemble(at, mine, one, two, three, out):
    width = mine.shape[-1]
    for e, got in enumerate((mine, one, two, three)):
        start = pl.multiple_of(lax.rem(at[1] + N - e, N) * width, 128)
        for a in range(2):
            out[a, :, pl.ds(start, width)] = got[a]


def second_products(at, mine, one, two, three, w_in, w_out, hidden, keep, send):
    block = mine.shape[1]
    half = block // 2
    for a in range(2):
        for d, got in enumerate((mine, one, two, three)):
            hidden[a, d * block : (d + 1) * block] = got[a]
    for a in range(2):
        if a == 0:
            part = dot(hidden[0], w_out[...], 1, 0)
        else:
            part = dot(hidden[1], w_in[...], 1, 1)
        for d in range(N):
            k = lax.rem(at[0] + N - d, N)
            keep[k, a] = part[d * block : d * block + half]
            send[k, a] = part[d * block + half : (d + 1) * block].astype(BF16)


def add_halves(keep, got, base, *outs):
    for k, out in enumerate((base, *outs)):
        out[...] = (keep[k] + got[k].astype(F32)).astype(out.dtype)


def add_all(base, *refs):
    total = base[...]
    for got in refs[:-1]:
        total = total + got[...].astype(F32)
    refs[-1][...] = total.astype(BF16)


def weight_grad(rows, hidden, *rest, of_rows):
    *before, out, lhs = rest
    which = 0 if of_rows else 1
    block = rows.shape[1] // N
    for d in range(N):
        f = (N - d) % N
        lhs[d * block : (d + 1) * block] = rows[which, f * block : (f + 1) * block]
    width = 256
    for n in range(out.shape[0] // width):
        cut = slice(n * width, (n + 1) * width)
        if of_rows:
            part = dot(lhs[:, cut], hidden[1], 0, 0)
        else:
            part = dot(hidden[0, :, cut], lhs[...], 0, 0)
        if before:
            part = part + before[0][cut, :]
        out[cut, :] = part.astype(out.dtype)


def own_sum(tokens, grad_out, base, *refs):
    *parts, out = refs
    for a, source in enumerate((tokens, grad_out)):
        total = source[...].astype(F32) + base[a]
        for part in parts:
            total = total + part[a].astype(F32)
        out[a] = total


def final_sum(base, got, output, grad_tokens):
    for a, out in enumerate((output, grad_tokens)):
        out[...] = base[a] + got[a].astype(F32)


def keep_as_is(source, out):
    out[...] = source[...]


def shift(value, axis, step):
    return lax.ppermute(value, axis, [(i, (i + step) % N) for i in range(N)])


def swap(value, axis):
    return lax.ppermute(value, axis, [(0, 1), (1, 0)])


def shards(tokens, w_in, w_out, grad_out):
    half, width = tokens.shape
    hidden = w_in.shape[1]
    block = 2 * half
    cut = hidden // N
    at = jnp.stack([lax.axis_index("x"), lax.axis_index("zl")]).astype(jnp.int32)
    order = Order()
    product_flops = 4 * N * block * width * hidden

    mine = jnp.stack([tokens, grad_out])

    def send(values, axis):
        return [shift(s, axis, d) for d, s in enumerate(values, 1)]

    def first(rows, after=()):
        rows, keep, *out = order.call(
            first_products,
            [((2, N * block, width), BF16), ((2, block, hidden), F32)]
            + [((2, block, hidden), BF16)] * 3,
            at, rows, swap(rows, "core"), w_in, w_out, after=after,
        )
        return rows, keep, send(out, "x")

    def add(keep, got):
        keep, *out = order.call(
            add_blocks,
            [((2, block, cut), F32)] + [((2, block, cut), BF16)] * 3,
            at, keep, *got,
        )
        return keep, send(out, "zl")

    def act(keep, got):
        return order.call(activate, [((2, block, cut), BF16)], keep, *got)[0]

    def spread(wide):
        return [wide] + send([wide] * 3, "x")

    def second(wide, after=()):
        hid, keep, out = order.call(
            second_products,
            [
                ((2, N * block, hidden), BF16),
                ((N, 2, half, width), F32),
                ((N, 2, half, width), BF16),
            ],
            at, *wide, w_in, w_out, after=after,
        )
        return hid, keep, out

    part = ((2, half, width), BF16)

    def halves(keep, got):
        base, *out = order.call(
            add_halves, [((2, half, width), F32)] + [part] * 3, keep, swap(got, "core")
        )
        return base, send(out, "y")

    def grad(shape, of_rows, dtype, rows, hid, *before):
        return order.call(
            functools.partial(weight_grad, of_rows=of_rows),
            [(shape, dtype)],
            rows, hid, *before,
            flops=product_flops // 2, traffic=8 << 20,
            scratch=[pltpu.VMEM(rows.shape[1:], BF16)],
        )[0]

    own = jnp.stack([mine] + [shift(mine, "y", -k) for k in range(1, N)])
    far = swap(own, "zh")
    rows_o, keep_o, got_o = first(own)
    (far,) = order.call(keep_as_is, [(far.shape, BF16)], far, after=got_o[:2])
    rows_f, keep_f, got_f = first(far, got_o)
    keep_o, got_o = add(keep_o, got_o)
    piece_o = act(keep_o, got_o)
    got_o = send([piece_o] * 3, "zl")
    keep_f, got_f = add(keep_f, got_f)
    (wide_o,) = order.call(
        assemble, [((2, block, hidden), BF16)], at, piece_o, *got_o
    )
    wide_o = spread(wide_o)
    piece_f = act(keep_f, got_f)
    got_f = send([piece_f] * 3, "zl")
    (wide_f,) = order.call(
        assemble, [((2, block, hidden), BF16)], at, piece_f, *got_f, after=wide_o[1:]
    )
    wide_f = spread(wide_f)
    hid_o, keep_o, got_o = second(wide_o)
    grad_in = grad((width, hidden), True, F32, rows_o, hid_o)
    grad_second = grad((hidden, width), False, F32, rows_o, hid_o)
    base, parts = halves(keep_o, got_o)
    (own_total,) = order.call(
        own_sum, [((2, half, width), F32)], tokens, grad_out, base, *parts
    )
    hid_f, keep_f, got_f = second(wide_f)
    base, parts = halves(keep_f, got_f)
    grad_in = grad((width, hidden), True, BF16, rows_f, hid_f, grad_in)
    (total,) = order.call(add_all, [part], base, *parts)
    got = swap(total, "zh")
    grad_second = grad((hidden, width), False, BF16, rows_f, hid_f, grad_second)
    output, grad_tokens = order.call(
        final_sum, [((half, width), F32)] * 2, own_total, got
    )
    return output, grad_tokens, grad_in, grad_second


def solution(mesh):
    fine = Mesh(mesh.devices.reshape(4, 2, 4, 4, 2), ("y", "core", "zl", "x", "zh"))
    row, col = ("y", "core", "zh"), ("zl", "x")
    by_token, in_spec, out_spec = P(row, col), P(col, row), P(row, col)
    return jax.shard_map(
        shards,
        mesh=fine,
        in_specs=(by_token, in_spec, out_spec, by_token),
        out_specs=(by_token, by_token, in_spec, out_spec),
        check_vma=False,
    )
```
